256 devices in a mesh: ctx: 64 (over x_lo, y, z), fsdp: 4 (over x_hi, core).
Axes of the slice: x: 4 (x_hi: 2, x_lo: 2; x = x_hi * 2 + x_lo), y: 4, z: 8, core: 2. Of those that a mesh axis runs over, the one named last changes fastest.
Arguments:
- query_rows: bfloat16 [8192, 2048], P('ctx', 'fsdp'), may hold values from -6 to 6
- key_rows: bfloat16 [8192, 2048], P('ctx', 'fsdp'), may hold values from -6 to 6
- value_rows: bfloat16 [8192, 2048], P('ctx', 'fsdp'), may hold values from -6 to 6
- out_proj: bfloat16 [2048, 4096], P('fsdp'), may hold values from -3 to 3
- cotangent: bfloat16 [8192, 4096], P('ctx', 'fsdp'), may hold values from -0.875 to 0.875
Outputs:
- layer_out: bfloat16 [8192, 4096], P('ctx', 'fsdp')
- grad_query: bfloat16 [8192, 2048], P('ctx', 'fsdp')
- grad_key: bfloat16 [8192, 2048], P('ctx', 'fsdp')
- grad_value: bfloat16 [8192, 2048], P('ctx', 'fsdp')
- proj_grad: float32 [4096, 2048], P('ctx', 'fsdp')
The draws below stay inside these ranges and needn't reach their ends.
All inputs are finite; a program needn't handle non-finite values.
Results may differ from the reference program's by a relative error of at most 0.015.
Values may be sent and summed in bfloat16 or wider, within the bound.
No kernel may reach another device: no remote copies, remote signals or barrier semaphores. Data moves between devices by JAX's collectives and lax.ppermute only.
A program may use at most 128 MiB of HBM per device.

```python
import math
import jax
import jax.numpy as jnp
from jax import lax

D = 4096
HEADS = 16
HEAD = 128
SEQ = 8192
HW = 2048


def draw_query_rows(key, part):
    key = jax.random.fold_in(key, 5)
    drawn_rows = jnp.clip(jax.random.normal(key, (SEQ, HEADS * HEAD), jnp.float32), -6.0, 6.0)
    return drawn_rows.astype(jnp.bfloat16)


def draw_key_rows(key, part):
    key = jax.random.fold_in(key, 7)
    drawn_rows = jnp.clip(jax.random.normal(key, (SEQ, HEADS * HEAD), jnp.float32), -6.0, 6.0)
    return drawn_rows.astype(jnp.bfloat16)


def strengthened(entries, stream_key, source, target, parts, factor):
    def block_of(dim):
        return (jnp.arange(entries.shape[dim]) // (entries.shape[dim] // parts)).reshape((-1,) + (1,) * (entries.ndim - 1 - dim))

    near = jax.random.permutation(stream_key, parts)[block_of(target)]
    far = (block_of(target) + parts // 2) % parts
    return jnp.where((block_of(source) == near) | (block_of(source) == far), factor * entries, entries)


def block_scale(key, extent, split, smallest, high):
    loudness = 1.0
    for axis_at, blocks in split:
        heights = jax.random.uniform(jax.random.fold_in(jax.random.fold_in(key, 6), axis_at), (blocks,), jnp.float32, smallest / len(split), high / len(split))
        loudness = loudness * jnp.repeat(jnp.exp(heights), extent[axis_at] // blocks).reshape((-1,) + (1,) * (len(extent) - 1 - axis_at))
    return loudness


def normal_values(stream_key, extent, scale, reach, pieces=(), held_as=jnp.bfloat16):
    array = jax.random.normal(stream_key, extent, jnp.float32) * scale
    if len(pieces) > 0:
        array = block_scale(stream_key, extent, pieces, -0.22, 0.18) * array
    return jnp.clip(array, min=-reach, max=reach).astype(held_as)


def heavy_noise(rng, extent, width, most, pieces, heavy, held_as=jnp.bfloat16):
    entries = width * jax.random.normal(rng, extent, jnp.float32)
    if pieces:
        entries = entries * block_scale(rng, extent, pieces, -0.22, 0.18)
    return jnp.clip(strengthened(entries, jax.random.fold_in(rng, 3), *heavy), -most, most).astype(held_as)


def setup_inputs(seed: int = 0) -> dict:
    key_of = jax.random.split(jax.random.key(seed), 6)
    return {
        "query_rows": draw_query_rows(jax.random.fold_in(key_of[5], 71), 0),
        "key_rows": draw_key_rows(jax.random.fold_in(key_of[5], 71), 0),
        "value_rows": normal_values(key_of[2], (SEQ, HW), 1.0, 6.0, ((0, 64), (1, 4))),
        "out_proj": normal_values(key_of[3], (HW, D), 0.5, 3.0, ((0, 4),)),
        "cotangent": heavy_noise(key_of[4], (SEQ, D), 0.05, 0.875, ((0, 64), (1, 4)), (0, 1, 64, 4.0)),
    }


NEG_BIG = -1e30


def split_heads(matrix):
    return matrix.reshape(SEQ, HEADS, HEAD).transpose(1, 0, 2)


def merge_heads(stacked):
    return stacked.transpose(1, 0, 2).reshape(SEQ, HEADS * HEAD)


def one_head(packed):
    q_head, k_head, v_head, do_head = packed
    score_scale = HEAD ** -0.5
    block_rows = math.gcd(SEQ, 1024)
    block_count = SEQ // block_rows
    col_pos = jnp.arange(SEQ)

    def query_block(carried, block_idx):
        dk_sum, dv_sum = carried
        row_start = (block_idx * block_rows).astype(jnp.int32)
        q_blk = lax.dynamic_slice_in_dim(q_head, row_start, block_rows, 0)
        do_blk = lax.dynamic_slice_in_dim(do_head, row_start, block_rows, 0)
        row_pos = row_start + jnp.arange(block_rows)
        allowed = col_pos[None, :] <= row_pos[:, None]
        scores = jnp.where(allowed, jnp.dot(q_blk, k_head.T, preferred_element_type=jnp.float32) * score_scale, NEG_BIG)
        row_top = jnp.max(scores, axis=1)
        row_total = jnp.sum(jnp.where(allowed, jnp.exp(scores - row_top[:, None]), 0.0), axis=1)
        log_total = row_top + jnp.log(row_total)
        weights = jnp.where(allowed, jnp.exp(scores - log_total[:, None]), 0.0)
        weights_bf = weights.astype(jnp.bfloat16)
        attended = jnp.dot(weights_bf, v_head, preferred_element_type=jnp.float32).astype(jnp.bfloat16)
        row_delta = jnp.sum(do_blk.astype(jnp.float32) * attended.astype(jnp.float32), axis=1)
        grad_prob = jnp.dot(do_blk, v_head.T, preferred_element_type=jnp.float32)
        dscore = (weights * (grad_prob - row_delta[:, None])).astype(jnp.bfloat16)
        dq_blk = (jnp.dot(dscore, k_head, preferred_element_type=jnp.float32) * score_scale).astype(jnp.bfloat16)
        dk_sum = dk_sum + jnp.dot(dscore.T, q_blk, preferred_element_type=jnp.float32) * score_scale
        dv_sum = dv_sum + jnp.dot(weights_bf.T, do_blk, preferred_element_type=jnp.float32)
        return (dk_sum, dv_sum), (attended, dq_blk)

    zeros_init = jnp.zeros((SEQ, HEAD), jnp.float32)
    (dk_sum, dv_sum), (attn_parts, dq_parts) = lax.scan(query_block, (zeros_init, zeros_init), jnp.arange(block_count))
    return (attn_parts.reshape(SEQ, HEAD), dq_parts.reshape(SEQ, HEAD),
            dk_sum.astype(jnp.bfloat16), dv_sum.astype(jnp.bfloat16))


def reference(query_rows, key_rows, value_rows, out_proj, cotangent):
    grad_attn = jnp.dot(cotangent, out_proj.T, preferred_element_type=jnp.float32).astype(jnp.bfloat16)
    per_head = lax.map(one_head, (split_heads(query_rows), split_heads(key_rows),
                                  split_heads(value_rows), split_heads(grad_attn)))
    attended = merge_heads(per_head[0])
    grad_query = merge_heads(per_head[1])
    grad_key = merge_heads(per_head[2])
    grad_value = merge_heads(per_head[3])
    layer_out = jnp.dot(attended, out_proj, preferred_element_type=jnp.float32).astype(jnp.bfloat16)
    proj_grad = jnp.dot(cotangent.T, attended, preferred_element_type=jnp.float32)
    return layer_out, grad_query, grad_key, grad_value, proj_grad
```

```python
import functools

import jax
import jax.numpy as jnp
from jax import lax
from jax.experimental import pallas as pl
from jax.experimental.pallas import tpu as pltpu
from jax.sharding import PartitionSpec as P

HEAD = 128
BLK = 128
SPAN = 4 * BLK
PIECE = BLK + 16
SCALE = HEAD ** -0.5
LOG2E = 1.4426950408889634
NEG_BIG = -1e30
F32 = jnp.float32
BF16 = jnp.bfloat16
VMEM_LIMIT = 48 * 1024 * 1024

NT = (((1,), (1,)), ((), ()))


def mm(lhs, rhs):
    return jnp.dot(lhs, rhs, preferred_element_type=F32)


def mm_nt(lhs, rhs):
    return lax.dot_general(lhs, rhs, NT, preferred_element_type=F32)


def spot(p, u, r):
    return 16 * p + 4 * u + r


def query_groups():
    return [
        [spot(p, a ^ (2 * (p & 1)), r) for p in range(4) for r in range(4)] for a in range(4)
    ]


def key_groups():
    return [[spot(p, u, r) for p in range(4) for u in range(4)] for r in range(4)]


def exchange(pieces, groups):
    return lax.all_to_all(pieces, "ctx", 0, 0, axis_index_groups=groups, tiled=True)


def fwd_kernel(place_ref, q_ref, kv_ref, o_ref, lse_ref, vt_ref, m_ref, l_ref, acc_ref):
    r_key = place_ref[4]
    for j in range(16):
        vt_ref[:, j * BLK : (j + 1) * BLK] = kv_ref[j, BLK:, :].T
    gap = lax.broadcasted_iota(jnp.int32, (BLK, SPAN), 1) - lax.broadcasted_iota(
        jnp.int32, (BLK, SPAN), 0
    )
    allowed = gap >= r_key * BLK

    def span(p, _):
        q = q_ref[pl.ds(4 * p, 4)].reshape(SPAN, HEAD)
        m_ref[...] = jnp.full((1, SPAN), NEG_BIG, F32)
        l_ref[...] = jnp.zeros((1, SPAN), F32)
        acc_ref[...] = jnp.zeros((HEAD, SPAN), F32)

        def chunk(j, count, masked):
            k = kv_ref[pl.ds(j, count), :BLK, :].reshape(count * BLK, HEAD)
            s = mm_nt(k, q) * (SCALE * LOG2E)
            if masked:
                s = jnp.where(allowed, s, NEG_BIG)
            m_old = m_ref[...]
            m_new = jnp.maximum(m_old, jnp.max(s, axis=0, keepdims=True))
            w = jnp.exp2(s - m_new)
            if masked:
                w = jnp.where(allowed, w, 0.0)
            alpha = jnp.exp2(m_old - m_new)
            m_ref[...] = m_new
            l_ref[...] = l_ref[...] * alpha + jnp.sum(w, axis=0, keepdims=True)
            cols = pl.ds(pl.multiple_of(j * BLK, BLK), count * BLK)
            acc_ref[...] = acc_ref[...] * alpha + mm(vt_ref[:, cols], w.astype(BF16))

        @pl.loop(0, p)
        def _(i):
            chunk(4 * i, 4, False)

        last = place_ref[p]

        @pl.loop(0, last)
        def _(i):
            chunk(4 * p + i, 1, False)

        chunk(4 * p + last, 1, True)

        total = l_ref[...]
        some = total > 0.0
        safe = jnp.where(some, total, 1.0)
        lse = jnp.where(some, m_ref[...] + jnp.log2(safe), NEG_BIG)
        out = acc_ref[...] * jnp.where(some, 1.0 / safe, 0.0)
        lse_ref[:, pl.ds(pl.multiple_of(p * SPAN, SPAN), SPAN)] = lse
        high = lse.astype(BF16)
        rest = lse - high.astype(F32)
        mid = rest.astype(BF16)
        low = (rest - mid.astype(F32)).astype(BF16)
        row = lax.broadcasted_iota(jnp.int32, (16, BLK), 0)
        for r in range(4):
            at = slice(r * BLK, (r + 1) * BLK)
            o_ref[4 * p + r, :BLK, :] = out[:, at].T.astype(BF16)
            three = jnp.where(
                row == 0,
                high[:, at].astype(F32),
                jnp.where(
                    row == 1,
                    mid[:, at].astype(F32),
                    jnp.where(row == 2, low[:, at].astype(F32), 0.0),
                ),
            )
            o_ref[4 * p + r, BLK:, :] = three.astype(BF16)
        return 0

    lax.fori_loop(0, 4, span, 0)


def delta_kernel(do_ref, o_ref, lse_ref, out_ref):
    out_ref[0:1, :] = lse_ref[...]
    for j in range(16):
        prod = do_ref[j].astype(F32) * o_ref[j, :BLK, :].astype(F32)
        out_ref[1:2, j * BLK : (j + 1) * BLK] = jnp.sum(prod.T, axis=0, keepdims=True)


def bwd_kernel(
    place_ref, q_ref, kv_ref, do_ref, st0, st1, st2, st3, dq_ref, dkv_ref, kt_ref, lse_ref, delta_ref,
    dqt_ref, dk_ref, dv_ref
):
    r_key = place_ref[4]
    stats = [st[...] for st in (st0, st1, st2, st3)]
    top = functools.reduce(jnp.maximum, [st[0:1] for st in stats])
    lse = top + jnp.log2(sum(jnp.exp2(st[0:1] - top) for st in stats))
    lse_ref[...] = lse
    delta_ref[...] = sum(jnp.exp2(st[0:1] - lse) * st[1:2] for st in stats)
    for j in range(16):
        kt_ref[:, j * BLK : (j + 1) * BLK] = kv_ref[j, :BLK, :].T
    dk_ref[...] = jnp.zeros_like(dk_ref)
    dv_ref[...] = jnp.zeros_like(dv_ref)
    gap = lax.broadcasted_iota(jnp.int32, (BLK, SPAN), 1) - lax.broadcasted_iota(
        jnp.int32, (BLK, SPAN), 0
    )
    allowed = gap >= r_key * BLK

    def span(p, _):
        q = q_ref[pl.ds(4 * p, 4)].reshape(SPAN, HEAD)
        do = do_ref[pl.ds(4 * p, 4)].reshape(SPAN, HEAD)
        here = pl.ds(pl.multiple_of(p * SPAN, SPAN), SPAN)
        lse_now = lse_ref[:, here]
        delta_now = delta_ref[:, here]
        dqt_ref[...] = jnp.zeros((HEAD, SPAN), F32)

        def chunk(j, count, masked):
            k = kv_ref[pl.ds(j, count), :BLK, :].reshape(count * BLK, HEAD)
            v = kv_ref[pl.ds(j, count), BLK:, :].reshape(count * BLK, HEAD)
            w = jnp.exp2(mm_nt(k, q) * (SCALE * LOG2E) - lse_now)
            if masked:
                w = jnp.where(allowed, w, 0.0)
            ds = (w * (mm_nt(v, do) - delta_now)).astype(BF16)
            rows = pl.ds(pl.multiple_of(j * BLK, BLK), count * BLK)
            dv_ref[rows, :] += mm(w.astype(BF16), do)
            dk_ref[rows, :] += mm(ds, q)
            dqt_ref[...] += mm(kt_ref[:, rows], ds)

        @pl.loop(0, p)
        def _(i):
            chunk(4 * i, 4, False)

        last = place_ref[p]

        @pl.loop(0, last)
        def _(i):
            chunk(4 * p + i, 1, False)

        chunk(4 * p + last, 1, True)
        for r in range(4):
            part = dqt_ref[:, r * BLK : (r + 1) * BLK] * SCALE
            dq_ref[4 * p + r] = part.T.astype(BF16)
        return 0

    lax.fori_loop(0, 4, span, 0)
    for j in range(16):
        at = slice(j * BLK, (j + 1) * BLK)
        dkv_ref[j, :BLK, :] = (dk_ref[at, :] * SCALE).astype(BF16)
        dkv_ref[j, BLK:, :] = dv_ref[at, :].astype(BF16)


def in_vmem(count):
    return [pl.BlockSpec(memory_space=pltpu.VMEM)] * count


def on_device(kernel, out_shape, scratch, smem, flops, moved):
    def call(*args):
        specs = [pl.BlockSpec(memory_space=pltpu.SMEM)] * smem + in_vmem(len(args) - smem)
        return pl.pallas_call(
            kernel,
            out_shape=out_shape,
            in_specs=specs,
            out_specs=jax.tree.map(lambda _: pl.BlockSpec(memory_space=pltpu.VMEM), out_shape),
            scratch_shapes=scratch,
            compiler_params=pltpu.CompilerParams(vmem_limit_bytes=VMEM_LIMIT),
            cost_estimate=pl.CostEstimate(flops=flops, bytes_accessed=moved, transcendentals=0),
        )(*args)

    return call


def per_device(query_rows, key_rows, value_rows, out_proj, cotangent):
    me = lax.axis_index("ctx")
    my_p, my_u, my_r = me // 16, (me // 4) % 4, me % 4
    spans = jnp.arange(4)
    last = my_u ^ (2 * ((spans ^ my_p) & 1))
    place = jnp.concatenate([last, my_r[None], jnp.zeros((3,), last.dtype)]).astype(jnp.int32)
    by_query, by_key = query_groups(), key_groups()

    def to_heads(rows):
        return rows.reshape(BLK, 4, HEAD).transpose(1, 0, 2)

    def four_times(per_head):
        shape = per_head.shape
        return jnp.broadcast_to(per_head[:, None], (4, 4) + shape[1:]).reshape((16,) + shape[1:])

    full_cot = lax.all_gather(cotangent, "fsdp", axis=1, tiled=True)
    kv = exchange(
        four_times(jnp.concatenate([to_heads(key_rows), to_heads(value_rows)], axis=1)), by_key
    )
    q = exchange(four_times(to_heads(query_rows)), by_query)

    tokens = 16 * BLK
    o_part, lse_part = on_device(
        fwd_kernel,
        (
            jax.ShapeDtypeStruct((16, PIECE, HEAD), BF16),
            jax.ShapeDtypeStruct((1, tokens), F32),
        ),
        [
            pltpu.VMEM((HEAD, tokens), BF16),
            pltpu.VMEM((1, SPAN), F32),
            pltpu.VMEM((1, SPAN), F32),
            pltpu.VMEM((HEAD, SPAN), F32),
        ],
        1,
        1_200_000_000,
        2_600_000,
    )(place, q, kv)

    o_home = exchange(o_part, by_query)
    rest = o_home[:, BLK : BLK + 3, :].astype(F32)
    totals = (rest[:, 0] + rest[:, 1] + rest[:, 2]).reshape(4, 4, BLK)
    top = jnp.max(totals, axis=1, keepdims=True)
    powers = jnp.exp2(totals - top)
    shares = powers / jnp.sum(powers, axis=1, keepdims=True)
    attended = jnp.sum(
        o_home[:, :BLK, :].astype(F32).reshape(4, 4, BLK, HEAD) * shares[..., None], axis=1
    )
    attended = attended.transpose(1, 0, 2).reshape(BLK, 4 * HEAD).astype(BF16)

    grad_attn = mm_nt(full_cot, out_proj).astype(BF16)
    do = exchange(four_times(to_heads(grad_attn)), by_query)
    stats = on_device(
        delta_kernel, jax.ShapeDtypeStruct((2, tokens), F32), [], 0, 1_000_000, 1_100_000
    )(do, o_part, lse_part)
    others = [lax.ppermute(stats, "ctx", [(i, i ^ b) for i in range(64)]) for b in (1, 2, 3)]

    dq_part, dkv_part = on_device(
        bwd_kernel,
        (
            jax.ShapeDtypeStruct((16, BLK, HEAD), BF16),
            jax.ShapeDtypeStruct((16, 2 * BLK, HEAD), BF16),
        ),
        [
            pltpu.VMEM((HEAD, tokens), BF16),
            pltpu.VMEM((1, tokens), F32),
            pltpu.VMEM((1, tokens), F32),
            pltpu.VMEM((HEAD, SPAN), F32),
            pltpu.VMEM((tokens, HEAD), F32),
            pltpu.VMEM((tokens, HEAD), F32),
        ],
        1,
        3_000_000_000,
        3_600_000,
    )(place, q, kv, do, stats, *others)
    dq_home = exchange(dq_part, by_query)
    dkv_home = exchange(dkv_part, by_key)

    def gathered(parts):
        summed = jnp.sum(parts.astype(F32).reshape(4, 4, BLK, HEAD), axis=1)
        return summed.transpose(1, 0, 2).reshape(BLK, 4 * HEAD).astype(BF16)

    grad_query = gathered(dq_home)
    grad_key = gathered(dkv_home[:, :BLK])
    grad_value = gathered(dkv_home[:, BLK:])

    partial = mm(attended, out_proj).astype(BF16)
    layer_out = lax.psum_scatter(partial, "fsdp", scatter_dimension=1, tiled=True)

    along = [[8 * i + z for i in range(8)] for z in range(8)]
    across = [[8 * i + z for z in range(8)] for i in range(8)]
    cot_cols = exchange(full_cot.reshape(BLK, 8, 512).transpose(1, 0, 2), along)
    att_rows = exchange(jnp.broadcast_to(attended[None], (8, BLK, 512)), along)
    proj_part = lax.dot_general(
        cot_cols.reshape(8 * BLK, 512),
        att_rows.reshape(8 * BLK, 512),
        (((0,), (0,)), ((), ())),
        preferred_element_type=F32,
    ).astype(BF16)
    proj_home = exchange(proj_part.reshape(8, 64, 512), across)
    proj_grad = jnp.sum(proj_home.astype(F32), axis=0)
    return (layer_out, grad_query, grad_key, grad_value, proj_grad)


def solution(mesh):
    spec = P("ctx", "fsdp")
    return jax.shard_map(
        per_device,
        mesh=mesh,
        in_specs=(spec, spec, spec, P("fsdp", None), spec),
        out_specs=(spec, spec, spec, spec, spec),
        check_vma=False,
    )
```

```python
import functools

import jax
import jax.numpy as jnp
from jax import lax
from jax.experimental import pallas as pl
from jax.experimental.pallas import tpu as pltpu
from jax.sharding import PartitionSpec as P

HEAD = 128
BLK = 128
SPAN = 4 * BLK
PIECE = BLK + 16
TOKENS = 16 * BLK
SCALE = HEAD ** -0.5
LOG2E = 1.4426950408889634
NEG_BIG = -1e30
F32 = jnp.float32
BF16 = jnp.bfloat16
VMEM_LIMIT = 40 * 1024 * 1024

HEAD_STEP = (0, 24, 32, 56)
ROW_STEP = (0, 2, 4, 6)


def key_groups():
    return [
        [16 * p + 8 * y + 2 * r + z for p in range(4) for y in range(2) for z in range(2)]
        for r in range(4)
    ]


def exchange(pieces, groups):
    return lax.all_to_all(pieces, "ctx", 0, 0, axis_index_groups=groups, tiled=True)


def hop(block, step):
    return lax.ppermute(block, "ctx", [(i, i ^ step) for i in range(64)])


def over_heads(blocks):
    return [blocks[0]] + [hop(blocks[x], HEAD_STEP[x]) for x in (1, 2, 3)]


def over_rows(blocks):
    return [blocks[0]] + [hop(blocks[x], ROW_STEP[x]) for x in (1, 2, 3)]


def cot_hop(block, y):
    route = []
    for c in range(64):
        for f in range(4):
            p = c // 16
            goal = (c % 16) ^ (8 * ((p ^ f) & 1))
            route.append((4 * c + f, 4 * (16 * f + goal) + (p ^ y)))
    return lax.ppermute(block, ("ctx", "fsdp"), route)


def mm(lhs, rhs):
    return jnp.dot(lhs, rhs, preferred_element_type=F32)


def mm_nt(lhs, rhs):
    return lax.dot_general(lhs, rhs, (((1,), (1,)), ((), ())), preferred_element_type=F32)


def block_at(index, size=BLK):
    return pl.ds(pl.multiple_of(index * size, size), size)


def prep_kernel(place, q_ref, k_ref, v_ref, q0, q1, q2, q3, kv_ref):
    p = place[0]
    for x, out in enumerate((q0, q1, q2, q3)):
        out[...] = q_ref[:, block_at(p ^ x)]
    for j in range(16):
        at = slice((j // 4) * HEAD, (j // 4 + 1) * HEAD)
        kv_ref[j, :BLK, :] = k_ref[:, at]
        kv_ref[j, BLK:, :] = v_ref[:, at]


def grad_attn_kernel(place, c0, c1, c2, c3, w_ref, g0, g1, g2, g3, acc_ref):
    step = pl.program_id(0)
    for x, cot in enumerate((c0, c1, c2, c3)):

        @pl.when(step == x)
        def _():
            term = mm_nt(cot[...], w_ref[...])
            acc_ref[...] = term if x == 0 else acc_ref[...] + term

    @pl.when(step == 3)
    def _():
        for x, out in enumerate((g0, g1, g2, g3)):
            out[...] = acc_ref[:, block_at(place[0] ^ x)].astype(BF16)


def sort_rows(place, parts, out_ref):
    for xr, part in enumerate(parts):
        for xp in range(4):
            out_ref[4 * (place[0] ^ xp) + (place[1] ^ xr)] = part[xp]


def causal(place):
    row = lax.broadcasted_iota(jnp.int32, (2 * BLK, SPAN), 0) + 2 * BLK * place[1]
    col = lax.broadcasted_iota(jnp.int32, (2 * BLK, SPAN), 1)
    col = 2 * BLK * (col // BLK) + BLK * place[2] + col % BLK
    return row <= col


def for_chunks(place, p, chunk):
    @pl.loop(0, p)
    def _(i):
        chunk(4 * i, 4, False)

    y = place[4 + p]

    @pl.loop(0, y)
    def _(i):
        chunk(4 * p, 2, False)

    chunk(4 * p + 2 * y, 2, True)


def fwd_kernel(
    place, qa, qb, qc, qd, kv_ref, o0, o1, o2, o3, lse_ref, q_ref, vt_ref, m_ref, l_ref, acc_ref
):
    sort_rows(place, (qa, qb, qc, qd), q_ref)
    for j in range(16):
        vt_ref[:, j * BLK : (j + 1) * BLK] = kv_ref[j, BLK:, :].T
    allowed = causal(place)

    def span(p, _):
        q = q_ref[pl.ds(4 * p, 4)].reshape(SPAN, HEAD)
        m_ref[...] = jnp.full((1, SPAN), NEG_BIG, F32)
        l_ref[...] = jnp.zeros((1, SPAN), F32)
        acc_ref[...] = jnp.zeros((HEAD, SPAN), F32)

        def chunk(j, count, masked):
            k = kv_ref[pl.ds(j, count), :BLK, :].reshape(count * BLK, HEAD)
            s = mm_nt(k, q) * (SCALE * LOG2E)
            if masked:
                s = jnp.where(allowed, s, NEG_BIG)
            m_old = m_ref[...]
            m_new = jnp.maximum(m_old, jnp.max(s, axis=0, keepdims=True))
            w = jnp.exp2(s - m_new)
            if masked:
                w = jnp.where(allowed, w, 0.0)
            alpha = jnp.exp2(m_old - m_new)
            m_ref[...] = m_new
            l_ref[...] = l_ref[...] * alpha + jnp.sum(w, axis=0, keepdims=True)
            cols = pl.ds(pl.multiple_of(j * BLK, BLK), count * BLK)
            acc_ref[...] = acc_ref[...] * alpha + mm(vt_ref[:, cols], w.astype(BF16))

        for_chunks(place, p, chunk)
        total = l_ref[...]
        some = total > 0.0
        safe = jnp.where(some, total, 1.0)
        lse = jnp.where(some, m_ref[...] + jnp.log2(safe), NEG_BIG)
        lse_ref[:, block_at(p, SPAN)] = lse
        acc_ref[...] = acc_ref[...] * jnp.where(some, 1.0 / safe, 0.0)
        row = lax.broadcasted_iota(jnp.int32, (16, BLK), 0)
        for x, out in enumerate((o0, o1, o2, o3)):
            r = place[1] ^ x
            out[p, :BLK, :] = acc_ref[:, block_at(r)].T.astype(BF16)
            total_here = lse_ref[:, block_at(4 * p + r)]
            high = total_here.astype(BF16).astype(F32)
            rest = total_here - high
            mid = rest.astype(BF16).astype(F32)
            three = jnp.where(
                row == 0,
                high,
                jnp.where(row == 1, mid, jnp.where(row == 2, rest - mid, 0.0)),
            )
            out[p, BLK:, :] = three.astype(BF16)
        return 0

    lax.fori_loop(0, 4, span, 0)


def merge_kernel(o0, o1, o2, o3, out_ref):
    parts = (o0, o1, o2, o3)
    for p in range(4):
        sums = []
        for part in parts:
            three = part[p, BLK:, :].astype(F32)
            sums.append(three[0:1] + three[1:2] + three[2:3])
        top = functools.reduce(jnp.maximum, sums)
        powers = [jnp.exp2(s - top) for s in sums]
        whole = sum(powers)
        merged = 0.0
        for part, power in zip(parts, powers):
            share = jnp.broadcast_to(power / whole, (BLK, HEAD)).T
            merged = merged + share * part[p, :BLK, :].astype(F32)
        out_ref[p] = merged.astype(BF16)


def delta_kernel(place, d0, d1, d2, d3, o0, o1, o2, o3, lse_ref, out_ref):
    out_ref[0:1, :] = lse_ref[...]
    for xr, (do, o) in enumerate(zip((d0, d1, d2, d3), (o0, o1, o2, o3))):
        for xp in range(4):
            p, r = place[0] ^ xp, place[1] ^ xr
            prod = do[xp].astype(F32) * o[p, :BLK, :].astype(F32)
            out_ref[1:2, block_at(4 * p + r)] = jnp.sum(prod.T, axis=0, keepdims=True)


def bwd_kernel(
    place, qa, qb, qc, qd, da, db, dc, dd, kv_ref, st0, st1, st2, st3, dq0, dq1, dq2, dq3, dkv_ref,
    q_ref, do_ref, kt_ref, lse_ref, delta_ref, dqt_ref, dk_ref, dv_ref
):
    sort_rows(place, (qa, qb, qc, qd), q_ref)
    sort_rows(place, (da, db, dc, dd), do_ref)
    stats = [st[...] for st in (st0, st1, st2, st3)]
    top = functools.reduce(jnp.maximum, [st[0:1] for st in stats])
    lse = top + jnp.log2(sum(jnp.exp2(st[0:1] - top) for st in stats))
    lse_ref[...] = lse
    delta_ref[...] = sum(jnp.exp2(st[0:1] - lse) * st[1:2] for st in stats)
    for j in range(16):
        kt_ref[:, j * BLK : (j + 1) * BLK] = kv_ref[j, :BLK, :].T
    dk_ref[...] = jnp.zeros_like(dk_ref)
    dv_ref[...] = jnp.zeros_like(dv_ref)
    allowed = causal(place)

    def span(p, _):
        q = q_ref[pl.ds(4 * p, 4)].reshape(SPAN, HEAD)
        do = do_ref[pl.ds(4 * p, 4)].reshape(SPAN, HEAD)
        lse_now = lse_ref[:, block_at(p, SPAN)]
        delta_now = delta_ref[:, block_at(p, SPAN)]
        dqt_ref[...] = jnp.zeros((HEAD, SPAN), F32)

        def chunk(j, count, masked):
            k = kv_ref[pl.ds(j, count), :BLK, :].reshape(count * BLK, HEAD)
            v = kv_ref[pl.ds(j, count), BLK:, :].reshape(count * BLK, HEAD)
            w = jnp.exp2(mm_nt(k, q) * (SCALE * LOG2E) - lse_now)
            if masked:
                w = jnp.where(allowed, w, 0.0)
            ds = (w * (mm_nt(v, do) - delta_now)).astype(BF16)
            rows = pl.ds(pl.multiple_of(j * BLK, BLK), count * BLK)
            dv_ref[rows, :] += mm(w.astype(BF16), do)
            dk_ref[rows, :] += mm(ds, q)
            dqt_ref[...] += mm(kt_ref[:, rows], ds)

        for_chunks(place, p, chunk)
        dqt_ref[...] = dqt_ref[...] * SCALE
        for x, out in enumerate((dq0, dq1, dq2, dq3)):
            out[p] = dqt_ref[:, block_at(place[1] ^ x)].T.astype(BF16)
        return 0

    lax.fori_loop(0, 4, span, 0)
    for j in range(16):
        at = slice(j * BLK, (j + 1) * BLK)
        dkv_ref[j, :BLK, :] = (dk_ref[at, :] * SCALE).astype(BF16)
        dkv_ref[j, BLK:, :] = dv_ref[at, :].astype(BF16)


def dq_sum_kernel(place, d0, d1, d2, d3, e0, e1, e2, e3):
    for x, out in enumerate((e0, e1, e2, e3)):
        p = place[0] ^ x
        out[...] = sum(part[p].astype(F32) for part in (d0, d1, d2, d3)).astype(BF16)


def grads_kernel(place, e0, e1, e2, e3, dkv_ref, dq_ref, dk_ref, dv_ref):
    for x, part in enumerate((e0, e1, e2, e3)):
        dq_ref[:, block_at(place[0] ^ x)] = part[...]
    for h in range(4):
        total = sum(dkv_ref[4 * h + i].astype(F32) for i in range(4)).astype(BF16)
        at = slice(h * HEAD, (h + 1) * HEAD)
        dk_ref[:, at] = total[:BLK]
        dv_ref[:, at] = total[BLK:]


def layer_kernel(place, a0, a1, a2, a3, w_ref, l0, l1, l2, l3, rows_ref):
    step = pl.program_id(0)

    @pl.when(step == 0)
    def _():
        for x, part in enumerate((a0, a1, a2, a3)):
            rows_ref[:, block_at(place[0] ^ x)] = part[place[0]]

    for x, out in enumerate((l0, l1, l2, l3)):

        @pl.when(step == x)
        def _():
            out[...] = mm(rows_ref[...], w_ref[...]).astype(BF16)


def proj_kernel(place, a0, a1, a2, a3, c0, c1, c2, c3, out_ref, att_ref, cot_ref):
    for x, part in enumerate((a0, a1, a2, a3)):
        for p in range(4):
            att_ref[p * BLK : (p + 1) * BLK, block_at(place[0] ^ x)] = part[p]
    for y, part in enumerate((c0, c1, c2, c3)):
        cot_ref[block_at(place[3] ^ y), :] = part[...]
    for i in range(4):
        at = slice(i * 256, (i + 1) * 256)
        total = lax.dot_general(
            cot_ref[:, at], att_ref[...], (((0,), (0,)), ((), ())), preferred_element_type=F32
        )
        out_ref[4 * i : 4 * i + 4] = total.astype(BF16).reshape(4, 64, 512)


def like(*shape, dtype=BF16):
    return jax.ShapeDtypeStruct(shape, dtype)


def params():
    return pltpu.CompilerParams(vmem_limit_bytes=VMEM_LIMIT)


def cost(flops, moved):
    return pl.CostEstimate(flops=int(flops), bytes_accessed=int(moved), transcendentals=0)


def on_device(kernel, out_shape, scratch, flops, moved, placed=True):
    def call(*args):
        specs = [pl.BlockSpec(memory_space=pltpu.VMEM)] * len(args)
        if placed:
            specs[0] = pl.BlockSpec(memory_space=pltpu.SMEM)
        return pl.pallas_call(
            kernel,
            out_shape=out_shape,
            in_specs=specs,
            out_specs=jax.tree.map(lambda _: pl.BlockSpec(memory_space=pltpu.VMEM), out_shape),
            scratch_shapes=scratch,
            compiler_params=params(),
            cost_estimate=cost(flops, moved),
        )(*args)

    return call


def by_columns(kernel, out_shape, scratch, flops):
    def call(place, *args):
        whole = pl.BlockSpec(memory_space=pltpu.VMEM)
        return pl.pallas_call(
            kernel,
            out_shape=out_shape,
            grid_spec=pltpu.PrefetchScalarGridSpec(
                num_scalar_prefetch=1,
                grid=(4,),
                in_specs=[whole] * (len(args) - 1)
                + [pl.BlockSpec((512, 1024), lambda i, at: (0, at[3] ^ i))],
                out_specs=[whole] * len(out_shape),
                scratch_shapes=scratch,
            ),
            compiler_params=params(),
            cost_estimate=cost(flops, 6_000_000),
        )(place, *args)

    return call


def per_device(query_rows, key_rows, value_rows, out_proj, cotangent):
    c, f = lax.axis_index("ctx"), lax.axis_index("fsdp")
    p, y, r, z = c // 16, (c // 8) % 2, (c // 2) % 4, c % 2
    place = jnp.stack([p, r, z, f] + [y ^ ((p ^ i) & 1) for i in range(4)]).astype(jnp.int32)
    four = [like(BLK, HEAD)] * 4
    stacks = [like(4, BLK, HEAD)] * 4

    cots = [cotangent] + [
        lax.ppermute(cotangent, "fsdp", [(i, i ^ x) for i in range(4)]) for x in (1, 2, 3)
    ]
    *q_pieces, kv_pieces = on_device(
        prep_kernel, four + [like(16, 2 * BLK, HEAD)], [], 1e6, 1.6e6
    )(place, query_rows, key_rows, value_rows)
    kv = exchange(kv_pieces, key_groups())
    q = over_rows([jnp.stack(over_heads(q_pieces))] * 4)

    do_pieces = by_columns(grad_attn_kernel, four, [pltpu.VMEM((BLK, 512), F32)], 5.4e8)(
        place, *cots, out_proj
    )
    do = over_rows([jnp.stack(over_heads(do_pieces))] * 4)

    *o_part, lse_part = on_device(
        fwd_kernel,
        [like(4, PIECE, HEAD)] * 4 + [like(1, TOKENS, dtype=F32)],
        [
            pltpu.VMEM((16, BLK, HEAD), BF16),
            pltpu.VMEM((HEAD, TOKENS), BF16),
            pltpu.VMEM((1, SPAN), F32),
            pltpu.VMEM((1, SPAN), F32),
            pltpu.VMEM((HEAD, SPAN), F32),
        ],
        2e9,
        2.6e6,
    )(place, *q, kv)

    att_mine = on_device(merge_kernel, like(4, BLK, HEAD), [], 1e6, 7e5, placed=False)(
        *over_rows(o_part)
    )
    stats = on_device(delta_kernel, like(2, TOKENS, dtype=F32), [], 1e6, 1.1e6)(
        place, *do, *o_part, lse_part
    )
    stats = over_rows([stats] * 4)
    att = over_heads([att_mine] * 4)

    *dq_part, dkv_part = on_device(
        bwd_kernel,
        stacks + [like(16, 2 * BLK, HEAD)],
        [
            pltpu.VMEM((16, BLK, HEAD), BF16),
            pltpu.VMEM((16, BLK, HEAD), BF16),
            pltpu.VMEM((HEAD, TOKENS), BF16),
            pltpu.VMEM((1, TOKENS), F32),
            pltpu.VMEM((1, TOKENS), F32),
            pltpu.VMEM((HEAD, SPAN), F32),
            pltpu.VMEM((TOKENS, HEAD), F32),
            pltpu.VMEM((TOKENS, HEAD), F32),
        ],
        5e9,
        3.6e6,
    )(place, *q, *do, kv, *stats)

    dkv_home = exchange(dkv_part, key_groups())
    dq_pieces = on_device(dq_sum_kernel, four, [], 1e6, 6e5)(place, *over_rows(dq_part))
    dq_home = over_heads(dq_pieces)
    grad_query, grad_key, grad_value = on_device(
        grads_kernel, [like(BLK, 512)] * 3, [], 1e6, 1.6e6
    )(place, *dq_home, dkv_home)

    layer_parts = by_columns(
        layer_kernel, [like(BLK, 1024)] * 4, [pltpu.VMEM((BLK, 512), BF16)], 5.4e8
    )(place, *att, out_proj)
    layer_all = [layer_parts[0]] + [
        lax.ppermute(layer_parts[x], "fsdp", [(i, i ^ x) for i in range(4)]) for x in (1, 2, 3)
    ]
    layer_out = sum(part.astype(F32) for part in layer_all).astype(BF16)

    cot_cols = [cot_hop(cotangent, i) for i in range(4)]
    proj_part = on_device(
        proj_kernel,
        like(16, 64, 512),
        [pltpu.VMEM((4 * BLK, 512), BF16), pltpu.VMEM((4 * BLK, 1024), BF16)],
        5.4e8,
        2.6e6,
    )(place, *att, *cot_cols)
    proj_home = exchange(proj_part, [[16 * i + j for j in range(16)] for i in range(4)])
    proj_grad = jnp.sum(proj_home.astype(F32), axis=0)
    return (layer_out, grad_query, grad_key, grad_value, proj_grad)


def solution(mesh):
    spec = P("ctx", "fsdp")
    return jax.shard_map(
        per_device,
        mesh=mesh,
        in_specs=(spec, spec, spec, P("fsdp", None), spec),
        out_specs=(spec, spec, spec, spec, spec),
        check_vma=False,
    )
```

```python
import functools

import jax
import jax.numpy as jnp
from jax import lax
from jax.experimental import pallas as pl
from jax.experimental.pallas import tpu as pltpu
from jax.sharding import PartitionSpec as P

HEAD = 128
BLK = 128
SPAN = 4 * BLK
TOKENS = 16 * BLK
SCALE = HEAD ** -0.5
LOG2E = 1.4426950408889634
NEG_BIG = -1e30
F32 = jnp.float32
BF16 = jnp.bfloat16
VMEM_LIMIT = 64 * 1024 * 1024

R, Z = 2, 1
HEAD_STEP = (0, 24, 32, 56)
ROW_STEP = (0, R, 2 * R, 3 * R)
HALVES = [(y, z) for y in range(2) for z in range(2)]


def device(p, y, r, z):
    return 16 * p + 8 * (y ^ (p & 1)) + R * r + Z * z


def key_groups():
    return [[device(p, y ^ (p & 1), r, z) for p in range(4) for y, z in HALVES] for r in range(4)]


def query_groups():
    return [[device(p, y, r, z) for p in range(4) for r in range(4)] for y, z in HALVES]


def z_groups():
    return [[8 * i + z for z in range(8)] for i in range(8)]


def xy_groups():
    return [[8 * i + z for i in range(8)] for z in range(8)]


def exchange(pieces, groups):
    return lax.all_to_all(pieces, "ctx", 0, 0, axis_index_groups=groups, tiled=True)


def hop(block, step):
    return lax.ppermute(block, "ctx", [(i, i ^ step) for i in range(64)])


def over_heads(blocks):
    return [blocks[0]] + [hop(blocks[x], HEAD_STEP[x]) for x in (1, 2, 3)]


def over_rows(blocks):
    return [blocks[0]] + [hop(blocks[x], ROW_STEP[x]) for x in (1, 2, 3)]


def mm(lhs, rhs):
    return jnp.dot(lhs, rhs, preferred_element_type=F32)


def mm_nt(lhs, rhs):
    return lax.dot_general(lhs, rhs, (((1,), (1,)), ((), ())), preferred_element_type=F32)


def block_at(index, size=BLK):
    return pl.ds(pl.multiple_of(index * size, size), size)


def fetch(src, dst, sem):
    copy = pltpu.make_async_copy(src, dst, sem)
    copy.start()
    return copy


def prep_kernel(place, q_ref, k_ref, v_ref, q0, q1, q2, q3, kv_ref):
    for x, out in enumerate((q0, q1, q2, q3)):
        out[...] = q_ref[:, block_at(place[0] ^ x)]
    for j in range(16):
        at = slice((j // 4) * HEAD, (j // 4 + 1) * HEAD)
        kv_ref[j, :BLK, :] = k_ref[:, at]
        kv_ref[j, BLK:, :] = v_ref[:, at]


def w_columns(place, w_hbm, w_ref, sem):
    return [
        fetch(w_hbm.at[:, block_at(place[3] ^ x, 1024)], w_ref.at[x], sem.at[x]) for x in range(4)
    ]


def grad_attn_kernel(
    place, c0, c1, c2, c3, w_hbm, do_hbm, cot_hbm, c_ref, w_ref, do_ref, c_sem, w_sem, out_sem
):
    cots = [fetch(c, c_ref.at[x], c_sem.at[x]) for x, c in enumerate((c0, c1, c2, c3))]
    columns = w_columns(place, w_hbm, w_ref, w_sem)
    total = 0.0
    outs = []
    for x in range(4):
        cots[x].wait()
        for half in range(2):
            outs.append(
                fetch(
                    c_ref.at[x, :, 512 * half : 512 * (half + 1)],
                    cot_hbm.at[2 * (place[3] ^ x) + half],
                    out_sem.at[2 * x + half],
                )
            )
        columns[x].wait()
        total = total + mm_nt(c_ref[x], w_ref[x])
    for j in range(16):
        at = slice((j // 4) * HEAD, (j // 4 + 1) * HEAD)
        do_ref[j] = total[:, at].astype(BF16)
    outs.append(fetch(do_ref, do_hbm, out_sem.at[8]))
    for out in outs:
        out.wait()


def sort_rows(place, parts, out_ref):
    for x, part in enumerate(parts):
        for i in range(4):
            out_ref[4 * (place[0] ^ i) + (place[1] ^ x)] = part[i]


def causal(place, p):
    row = lax.broadcasted_iota(jnp.int32, (SPAN, SPAN), 0)
    row = (
        8 * BLK * (row // (2 * BLK)) + Z * BLK * (row // BLK % 2) + R * BLK * place[1] + row % BLK
    )
    col = lax.broadcasted_iota(jnp.int32, (1, SPAN), 1)
    col = R * BLK * (col // BLK) + BLK * (8 * place[4 + p] + Z * place[2]) + col % BLK
    return row <= col


def fwd_kernel(place, qa, qb, qc, qd, kv_ref, o0, o1, o2, o3, lse_ref, q_ref, vt_ref, out_ref):
    sort_rows(place, (qa, qb, qc, qd), q_ref)
    for j in range(16):
        vt_ref[:, j * BLK : (j + 1) * BLK] = kv_ref[j, BLK:, :].T
    for p in range(4):
        q = q_ref[4 * p : 4 * p + 4].reshape(SPAN, HEAD)
        mask = causal(place, p)
        scores = []
        for i in range(p + 1):
            k = kv_ref[4 * i : 4 * i + 4, :BLK, :].reshape(SPAN, HEAD)
            s = mm_nt(k, q) * (SCALE * LOG2E)
            scores.append(jnp.where(mask, s, NEG_BIG) if i == p else s)
        top = functools.reduce(jnp.maximum, [jnp.max(s, axis=0, keepdims=True) for s in scores])
        total, out = 0.0, 0.0
        for i, s in enumerate(scores):
            w = jnp.exp2(s - top)
            if i == p:
                w = jnp.where(mask, w, 0.0)
            total = total + jnp.sum(w, axis=0, keepdims=True)
            out = out + mm(vt_ref[:, i * SPAN : (i + 1) * SPAN], w.astype(BF16))
        some = total > 0.0
        safe = jnp.where(some, total, 1.0)
        lse = jnp.where(some, top + jnp.log2(safe), NEG_BIG)
        out_ref[...] = out * jnp.where(some, 1.0 / safe, 0.0)
        for r in range(4):
            lse_ref[4 * p + r : 4 * p + r + 1, :] = lse[:, r * BLK : (r + 1) * BLK]
        for x, to in enumerate((o0, o1, o2, o3)):
            to[p] = out_ref[:, block_at(place[1] ^ x)].T.astype(BF16)


def three_parts(value):
    high = value.astype(BF16)
    rest = value - high.astype(F32)
    mid = rest.astype(BF16)
    return high, mid, (rest - mid.astype(F32)).astype(BF16)


def pack_kernel(place, do_ref, o0, o1, o2, o3, lse_ref, p0, p1, p2, p3, delta_ref):
    for x, out in enumerate((o0, o1, o2, o3)):
        for p in range(4):
            j = 4 * p + (place[1] ^ x)
            prod = do_ref[j].astype(F32) * out[p].astype(F32)
            delta_ref[pl.ds(j, 1), :] = jnp.sum(prod.T, axis=0, keepdims=True)
    parts = three_parts(lse_ref[...]) + three_parts(delta_ref[...])
    for pack, out in zip((p0, p1, p2, p3), (o0, o1, o2, o3)):
        pack[:SPAN, :] = out[...].reshape(SPAN, HEAD)
        for i, part in enumerate(parts):
            pack[SPAN + 16 * i : SPAN + 16 * (i + 1), :] = part


def unpacked(pack, which):
    at = SPAN + 48 * which
    parts = [pack[at + 16 * i : at + 16 * (i + 1), :].astype(F32) for i in range(3)]
    return parts[0] + parts[1] + parts[2]


def log_totals(parts):
    top = functools.reduce(jnp.maximum, parts)
    return top + jnp.log2(sum(jnp.exp2(part - top) for part in parts))


def merge_kernel(place, p0, p1, p2, p3, out_ref, share_ref):
    packs = (p0, p1, p2, p3)
    parts = [unpacked(pack, 0) for pack in packs]
    total = log_totals(parts)
    for i, part in enumerate(parts):
        share_ref[i] = jnp.exp2(part - total)
    for p in range(4):
        merged = 0.0
        for i, pack in enumerate(packs):
            share = share_ref[i, pl.ds(4 * p + place[1], 1), :]
            share = jnp.broadcast_to(share, (BLK, HEAD)).T
            merged = merged + share * pack[p * BLK : (p + 1) * BLK, :].astype(F32)
        out_ref[p] = merged.astype(BF16)


def bwd_kernel(
    place, qa, qb, qc, qd, do_ref, kv_ref, p0, p1, p2, p3, dq0, dq1, dq2, dq3, dkv_ref,
    q_ref, kt_ref, lse_ref, delta_ref, dqt_ref, dk_ref, dv_ref
):
    sort_rows(place, (qa, qb, qc, qd), q_ref)
    parts = [unpacked(pack, 0) for pack in (p0, p1, p2, p3)]
    lse = log_totals(parts)
    lse_ref[...] = lse
    deltas = [unpacked(pack, 1) for pack in (p0, p1, p2, p3)]
    delta_ref[...] = sum(jnp.exp2(part - lse) * delta for part, delta in zip(parts, deltas))
    for j in range(16):
        kt_ref[:, j * BLK : (j + 1) * BLK] = kv_ref[j, :BLK, :].T
    for p in range(4):
        q = q_ref[4 * p : 4 * p + 4].reshape(SPAN, HEAD)
        do = do_ref[4 * p : 4 * p + 4].reshape(SPAN, HEAD)
        lse_now = jnp.concatenate([lse_ref[4 * p + r : 4 * p + r + 1, :] for r in range(4)], axis=1)
        delta_now = jnp.concatenate(
            [delta_ref[4 * p + r : 4 * p + r + 1, :] for r in range(4)], axis=1
        )
        dqt = 0.0
        for i in range(p + 1):
            rows = slice(i * SPAN, (i + 1) * SPAN)
            k = kv_ref[4 * i : 4 * i + 4, :BLK, :].reshape(SPAN, HEAD)
            v = kv_ref[4 * i : 4 * i + 4, BLK:, :].reshape(SPAN, HEAD)
            w = jnp.exp2(mm_nt(k, q) * (SCALE * LOG2E) - lse_now)
            if i == p:
                w = jnp.where(causal(place, p), w, 0.0)
            ds = (w * (mm_nt(v, do) - delta_now)).astype(BF16)
            dv, dk = mm(w.astype(BF16), do), mm(ds, q)
            dv_ref[rows, :] = dv if i == p else dv_ref[rows, :] + dv
            dk_ref[rows, :] = dk if i == p else dk_ref[rows, :] + dk
            dqt = dqt + mm(kt_ref[:, rows], ds)
        dqt_ref[...] = dqt * SCALE
        for x, out in enumerate((dq0, dq1, dq2, dq3)):
            out[p] = dqt_ref[:, block_at(place[1] ^ x)].T.astype(BF16)
    for j in range(16):
        at = slice(j * BLK, (j + 1) * BLK)
        dkv_ref[j, :BLK, :] = (dk_ref[at, :] * SCALE).astype(BF16)
        dkv_ref[j, BLK:, :] = dv_ref[at, :].astype(BF16)


def dq_sum_kernel(place, d0, d1, d2, d3, e0, e1, e2, e3):
    for x, out in enumerate((e0, e1, e2, e3)):
        p = place[0] ^ x
        out[...] = sum(part[p].astype(F32) for part in (d0, d1, d2, d3)).astype(BF16)


def last_kernel(
    place, e0, e1, e2, e3, dkv_ref, mine_ref, far_ref, proj_ref,
    layer_ref, dq_ref, dk_ref, dv_ref, sum_ref
):
    for x, part in enumerate((e0, e1, e2, e3)):
        dq_ref[:, block_at(place[0] ^ x)] = part[...]
    for h in range(4):
        total = sum(dkv_ref[4 * h + i].astype(F32) for i in range(4)).astype(BF16)
        at = slice(h * HEAD, (h + 1) * HEAD)
        dk_ref[:, at] = total[:BLK]
        dv_ref[:, at] = total[BLK:]
    layer_ref[...] = (mine_ref[...] + far_ref[...].astype(F32)).astype(BF16)
    sum_ref[...] = sum(proj_ref[i].astype(F32) for i in range(8))


def layer_kernel(
    place, a0, a1, a2, a3, w_hbm, kept_hbm, given_hbm, a_ref, rows_ref, w_ref, out_ref,
    a_sem, w_sem, out_sem
):
    parts = [fetch(a.at[place[0]], a_ref.at[x], a_sem.at[x]) for x, a in enumerate((a0, a1, a2, a3))]
    columns = w_columns(place, w_hbm, w_ref, w_sem)
    for x in range(4):
        parts[x].wait()
        rows_ref[:, block_at(place[0] ^ x)] = a_ref[x]
    outs = []
    for x in range(4):
        columns[x].wait()
        out_ref[x] = mm(rows_ref[...], w_ref[x]).astype(BF16)
        out = given_hbm if x & 1 else kept_hbm
        outs.append(fetch(out_ref.at[x], out.at[x >> 1], out_sem.at[x]))
    for out in outs:
        out.wait()


def pair_kernel(place, kept_ref, come_ref, mine_ref, other_ref):
    total = kept_ref[...].astype(F32) + come_ref[...].astype(F32)
    mine_ref[...] = total[0]
    other_ref[...] = total[1].astype(BF16)


def proj_kernel(place, a0, a1, a2, a3, others, cot_ref, out_ref, att_ref):
    for x, part in enumerate((a0, a1, a2, a3)):
        for p in range(4):
            cols = block_at(place[0] ^ x)
            att_ref[block_at(2 * p + place[4 + p]), cols] = part[p]
            att_ref[block_at(2 * p + (place[4 + p] ^ 1)), cols] = others[x, p]
    cot = cot_ref[...].reshape(8 * BLK, 512)
    for i in range(2):
        at = slice(i * 256, (i + 1) * 256)
        total = lax.dot_general(
            cot[:, at], att_ref[...], (((0,), (0,)), ((), ())), preferred_element_type=F32
        )
        out_ref[4 * i : 4 * i + 4] = total.astype(BF16).reshape(4, 64, 512)


def like(*shape, dtype=BF16):
    return jax.ShapeDtypeStruct(shape, dtype)


def params():
    return pltpu.CompilerParams(vmem_limit_bytes=VMEM_LIMIT)


def cost(flops, moved):
    return pl.CostEstimate(flops=int(flops), bytes_accessed=int(moved), transcendentals=0)


def raw(kernel, out_shape, scratch, flops, moved):
    def call(place, *args):
        return pl.pallas_call(
            kernel,
            out_shape=out_shape,
            in_specs=[pl.BlockSpec(memory_space=pltpu.SMEM)]
            + [pl.BlockSpec(memory_space=pltpu.HBM)] * len(args),
            out_specs=[pl.BlockSpec(memory_space=pltpu.HBM)] * len(out_shape),
            scratch_shapes=scratch,
            compiler_params=params(),
            cost_estimate=cost(flops, moved),
        )(place, *args)

    return call


def on_device(kernel, out_shape, scratch, flops, moved):
    def call(place, *args):
        return pl.pallas_call(
            kernel,
            out_shape=out_shape,
            in_specs=[pl.BlockSpec(memory_space=pltpu.SMEM)]
            + [pl.BlockSpec(memory_space=pltpu.VMEM)] * len(args),
            out_specs=[pl.BlockSpec(memory_space=pltpu.VMEM)] * len(out_shape),
            scratch_shapes=scratch,
            compiler_params=params(),
            cost_estimate=cost(flops, moved),
        )(place, *args)

    return call


def per_device(query_rows, key_rows, value_rows, out_proj, cotangent):
    c, f = lax.axis_index("ctx"), lax.axis_index("fsdp")
    p, y, r, z = c // 16, (c // 8) % 2, (c // 2) % 4, c % 2
    place = jnp.stack([p, r, z, f] + [y ^ ((p ^ i) & 1) for i in range(4)]).astype(jnp.int32)
    four = [like(BLK, HEAD)] * 4

    def swap(block, x):
        return lax.ppermute(block, "fsdp", [(i, i ^ x) for i in range(4)])

    far = swap(cotangent, 2)
    *q_pieces, kv_pieces = on_device(prep_kernel, four + [like(16, 2 * BLK, HEAD)], [], 1e6, 2e6)(
        place, query_rows, key_rows, value_rows
    )
    q_mine = jnp.stack(over_heads(q_pieces))
    kv_pieces, far, q_mine = lax.optimization_barrier((kv_pieces, far, q_mine))
    kv = exchange(kv_pieces, key_groups())
    q = over_rows([q_mine] * 4)
    cots = [cotangent, swap(cotangent, 1), far, swap(far, 1)]

    do_pieces, cot_pieces = raw(
        grad_attn_kernel,
        [like(16, BLK, HEAD), like(8, BLK, 512)],
        [
            pltpu.VMEM((4, BLK, 1024), BF16),
            pltpu.VMEM((4, 512, 1024), BF16),
            pltpu.VMEM((16, BLK, HEAD), BF16),
            pltpu.SemaphoreType.DMA((4,)),
            pltpu.SemaphoreType.DMA((4,)),
            pltpu.SemaphoreType.DMA((9,)),
        ],
        5.4e8,
        7e6,
    )(place, *cots, out_proj)
    do_pieces, kv, q = lax.optimization_barrier((do_pieces, kv, q))
    do = exchange(do_pieces, query_groups())

    *o_part, lse_part = on_device(
        fwd_kernel,
        [like(4, BLK, HEAD)] * 4 + [like(16, BLK, dtype=F32)],
        [
            pltpu.VMEM((16, BLK, HEAD), BF16),
            pltpu.VMEM((HEAD, TOKENS), BF16),
            pltpu.VMEM((HEAD, SPAN), F32),
        ],
        2e9,
        2.6e6,
    )(place, *q, kv)

    packs = on_device(
        pack_kernel, [like(SPAN + 96, HEAD)] * 4, [pltpu.VMEM((16, BLK), F32)], 1e6, 1.6e6
    )(place, do, *o_part, lse_part)
    packs, cot_pieces = lax.optimization_barrier((packs, cot_pieces))
    packs = over_rows(packs)
    (att_mine,) = on_device(
        merge_kernel, [like(4, BLK, HEAD)], [pltpu.VMEM((4, 16, BLK), F32)], 1e6, 7e5
    )(place, *packs)
    cot_cols = exchange(cot_pieces, xy_groups())
    packs, att_mine, cot_cols = lax.optimization_barrier((packs, att_mine, cot_cols))
    att = over_heads([att_mine] * 4)

    *dq_part, dkv_part = on_device(
        bwd_kernel,
        [like(4, BLK, HEAD)] * 4 + [like(16, 2 * BLK, HEAD)],
        [
            pltpu.VMEM((16, BLK, HEAD), BF16),
            pltpu.VMEM((HEAD, TOKENS), BF16),
            pltpu.VMEM((16, BLK), F32),
            pltpu.VMEM((16, BLK), F32),
            pltpu.VMEM((HEAD, SPAN), F32),
            pltpu.VMEM((TOKENS, HEAD), F32),
            pltpu.VMEM((TOKENS, HEAD), F32),
        ],
        5e9,
        3.6e6,
    )(place, *q, do, kv, *packs)

    att, cot_cols, dkv_part = lax.optimization_barrier((att, cot_cols, dkv_part))
    dkv_home = exchange(dkv_part, key_groups())
    kept, given = raw(
        layer_kernel,
        [like(2, BLK, 1024)] * 2,
        [
            pltpu.VMEM((4, BLK, HEAD), BF16),
            pltpu.VMEM((BLK, 512), BF16),
            pltpu.VMEM((4, 512, 1024), BF16),
            pltpu.VMEM((4, BLK, 1024), BF16),
            pltpu.SemaphoreType.DMA((4,)),
            pltpu.SemaphoreType.DMA((4,)),
            pltpu.SemaphoreType.DMA((4,)),
        ],
        5.4e8,
        6e6,
    )(place, *att, out_proj)
    (proj_part,) = on_device(
        proj_kernel, [like(8, 64, 512)], [pltpu.VMEM((8 * BLK, 512), BF16)], 5.4e8, 2.6e6
    )(place, *att, hop(jnp.stack(att), 8), cot_cols)
    dq_all = over_rows(dq_part)
    dq_all, proj_part, kept = lax.optimization_barrier((dq_all, proj_part, kept))

    mine, other = on_device(
        pair_kernel, [like(BLK, 1024, dtype=F32), like(BLK, 1024)], [], 1e6, 2e6
    )(place, kept, swap(given, 1))

    proj_part, dkv_home, dq_all = lax.optimization_barrier((proj_part, dkv_home, dq_all))
    proj_home = exchange(proj_part, z_groups())
    dq_pieces = on_device(dq_sum_kernel, four, [], 1e6, 6e5)(place, *dq_all)
    dq_home = over_heads(dq_pieces)
    layer_out, grad_query, grad_key, grad_value, proj_grad = on_device(
        last_kernel,
        [like(BLK, 1024)] + [like(BLK, 512)] * 3 + [like(64, 512, dtype=F32)],
        [],
        1e6,
        3.6e6,
    )(place, *dq_home, dkv_home, mine, swap(other, 2), proj_home)
    return (layer_out, grad_query, grad_key, grad_value, proj_grad)


def solution(mesh):
    spec = P("ctx", "fsdp")
    return jax.shard_map(
        per_device,
        mesh=mesh,
        in_specs=(spec, spec, spec, P("fsdp", None), spec),
        out_specs=(spec, spec, spec, spec, spec),
        check_vma=False,
    )
```

```python
import functools

import jax
import jax.numpy as jnp
from jax import lax
from jax.experimental import pallas as pl
from jax.experimental.pallas import tpu as pltpu
from jax.sharding import PartitionSpec as P

HEAD = 128
BLK = 128
SPAN = 4 * BLK
TOKENS = 16 * BLK
SCALE = HEAD ** -0.5
LOG2E = 1.4426950408889634
NEG_BIG = -1e30
F32 = jnp.float32
BF16 = jnp.bfloat16
VMEM_LIMIT = 64 * 1024 * 1024

R, Z = 2, 1
HEAD_STEP = (0, 24, 32, 56)
ROW_STEP = (0, R, 2 * R, 3 * R)
HALVES = [(y, z) for y in range(2) for z in range(2)]


def device(p, y, r, z):
    return 16 * p + 8 * (y ^ (p & 1)) + R * r + Z * z


def key_groups():
    return [[device(p, y ^ (p & 1), r, z) for p in range(4) for y, z in HALVES] for r in range(4)]


def query_groups():
    return [[device(p, y, r, z) for p in range(4) for r in range(4)] for y, z in HALVES]


def z_groups():
    return [[8 * i + z for z in range(8)] for i in range(8)]


def xy_groups():
    return [[8 * i + z for i in range(8)] for z in range(8)]


def exchange(pieces, groups):
    return lax.all_to_all(pieces, "ctx", 0, 0, axis_index_groups=groups, tiled=True)


def hop(block, step):
    return lax.ppermute(block, "ctx", [(i, i ^ step) for i in range(64)])


def over_heads(blocks):
    return [blocks[0]] + [hop(blocks[x], HEAD_STEP[x]) for x in (1, 2, 3)]


def over_rows(blocks):
    return [blocks[0]] + [hop(blocks[x], ROW_STEP[x]) for x in (1, 2, 3)]


def mm(lhs, rhs):
    return jnp.dot(lhs, rhs, preferred_element_type=F32)


def mm_nt(lhs, rhs):
    return lax.dot_general(lhs, rhs, (((1,), (1,)), ((), ())), preferred_element_type=F32)


def block_at(index, size=BLK):
    return pl.ds(pl.multiple_of(index * size, size), size)


def fetch(src, dst, sem):
    copy = pltpu.make_async_copy(src, dst, sem)
    copy.start()
    return copy


def prep_kernel(place, q_ref, k_ref, v_ref, q0, q1, q2, q3, kv_ref):
    for x, out in enumerate((q0, q1, q2, q3)):
        out[...] = q_ref[:, block_at(place[0] ^ x)]
    for j in range(16):
        at = slice((j // 4) * HEAD, (j // 4 + 1) * HEAD)
        kv_ref[j, :BLK, :] = k_ref[:, at]
        kv_ref[j, BLK:, :] = v_ref[:, at]


def w_columns(place, w_hbm, w_ref, sem):
    return [
        fetch(w_hbm.at[:, block_at(place[3] ^ x, 1024)], w_ref.at[x], sem.at[x]) for x in range(4)
    ]


def grad_attn_kernel(
    place, c0, c1, c2, c3, w_hbm, do_hbm, cot_hbm, c_ref, w_ref, do_ref, c_sem, w_sem, out_sem
):
    cots = [fetch(c, c_ref.at[x], c_sem.at[x]) for x, c in enumerate((c0, c1, c2, c3))]
    columns = w_columns(place, w_hbm, w_ref, w_sem)
    total = 0.0
    outs = []
    for x in range(4):
        cots[x].wait()
        for half in range(2):
            outs.append(
                fetch(
                    c_ref.at[x, :, 512 * half : 512 * (half + 1)],
                    cot_hbm.at[2 * (place[3] ^ x) + half],
                    out_sem.at[2 * x + half],
                )
            )
        columns[x].wait()
        total = total + mm_nt(c_ref[x], w_ref[x])
    for j in range(16):
        at = slice((j // 4) * HEAD, (j // 4 + 1) * HEAD)
        do_ref[j] = total[:, at].astype(BF16)
    outs.append(fetch(do_ref, do_hbm, out_sem.at[8]))
    for out in outs:
        out.wait()


def sort_rows(place, parts, out_ref):
    for x, part in enumerate(parts):
        for i in range(4):
            out_ref[4 * (place[0] ^ i) + (place[1] ^ x)] = part[i]


def causal(place, p):
    row = lax.broadcasted_iota(jnp.int32, (SPAN, SPAN), 0)
    row = (
        8 * BLK * (row // (2 * BLK)) + Z * BLK * (row // BLK % 2) + R * BLK * place[1] + row % BLK
    )
    col = lax.broadcasted_iota(jnp.int32, (1, SPAN), 1)
    col = R * BLK * (col // BLK) + BLK * (8 * place[4 + p] + Z * place[2]) + col % BLK
    return row <= col


def fwd_kernel(place, qa, qb, qc, qd, kv_ref, o0, o1, o2, o3, lse_ref, q_ref, vt_ref, out_ref):
    sort_rows(place, (qa, qb, qc, qd), q_ref)
    for j in range(16):
        vt_ref[:, j * BLK : (j + 1) * BLK] = kv_ref[j, BLK:, :].T
    for p in range(4):
        q = q_ref[4 * p : 4 * p + 4].reshape(SPAN, HEAD)
        mask = causal(place, p)
        scores = []
        for i in range(p + 1):
            k = kv_ref[4 * i : 4 * i + 4, :BLK, :].reshape(SPAN, HEAD)
            s = mm_nt(k, q) * (SCALE * LOG2E)
            scores.append(jnp.where(mask, s, NEG_BIG) if i == p else s)
        top = functools.reduce(jnp.maximum, [jnp.max(s, axis=0, keepdims=True) for s in scores])
        total, out = 0.0, 0.0
        for i, s in enumerate(scores):
            w = jnp.exp2(s - top)
            if i == p:
                w = jnp.where(mask, w, 0.0)
            total = total + jnp.sum(w, axis=0, keepdims=True)
            out = out + mm(vt_ref[:, i * SPAN : (i + 1) * SPAN], w.astype(BF16))
        some = total > 0.0
        safe = jnp.where(some, total, 1.0)
        lse = jnp.where(some, top + jnp.log2(safe), NEG_BIG)
        out_ref[...] = out * jnp.where(some, 1.0 / safe, 0.0)
        for r in range(4):
            lse_ref[4 * p + r : 4 * p + r + 1, :] = lse[:, r * BLK : (r + 1) * BLK]
        for x, to in enumerate((o0, o1, o2, o3)):
            to[p] = out_ref[:, block_at(place[1] ^ x)].T.astype(BF16)


def three_parts(value):
    high = value.astype(BF16)
    rest = value - high.astype(F32)
    mid = rest.astype(BF16)
    return high, mid, (rest - mid.astype(F32)).astype(BF16)


def pack_kernel(place, do_ref, o0, o1, o2, o3, lse_ref, p0, p1, p2, p3, delta_ref):
    for x, out in enumerate((o0, o1, o2, o3)):
        for p in range(4):
            j = 4 * p + (place[1] ^ x)
            prod = do_ref[j].astype(F32) * out[p].astype(F32)
            delta_ref[pl.ds(j, 1), :] = jnp.sum(prod.T, axis=0, keepdims=True)
    parts = three_parts(lse_ref[...]) + three_parts(delta_ref[...])
    for pack, out in zip((p0, p1, p2, p3), (o0, o1, o2, o3)):
        pack[:SPAN, :] = out[...].reshape(SPAN, HEAD)
        for i, part in enumerate(parts):
            pack[SPAN + 16 * i : SPAN + 16 * (i + 1), :] = part


def unpacked(pack, which):
    at = SPAN + 48 * which
    parts = [pack[at + 16 * i : at + 16 * (i + 1), :].astype(F32) for i in range(3)]
    return parts[0] + parts[1] + parts[2]


def log_totals(parts):
    top = functools.reduce(jnp.maximum, parts)
    return top + jnp.log2(sum(jnp.exp2(part - top) for part in parts))


def merge_kernel(place, p0, p1, p2, p3, out_ref, share_ref):
    packs = (p0, p1, p2, p3)
    parts = [unpacked(pack, 0) for pack in packs]
    total = log_totals(parts)
    for i, part in enumerate(parts):
        share_ref[i] = jnp.exp2(part - total)
    for p in range(4):
        merged = 0.0
        for i, pack in enumerate(packs):
            share = share_ref[i, pl.ds(4 * p + place[1], 1), :]
            share = jnp.broadcast_to(share, (BLK, HEAD)).T
            merged = merged + share * pack[p * BLK : (p + 1) * BLK, :].astype(F32)
        out_ref[p] = merged.astype(BF16)


def bwd_kernel(
    place, qa, qb, qc, qd, do_ref, kv_ref, p0, p1, p2, p3, dq0, dq1, dq2, dq3, dkv_ref,
    q_ref, kt_ref, lse_ref, delta_ref, dqt_ref, dk_ref, dv_ref
):
    sort_rows(place, (qa, qb, qc, qd), q_ref)
    parts = [unpacked(pack, 0) for pack in (p0, p1, p2, p3)]
    lse = log_totals(parts)
    lse_ref[...] = lse
    deltas = [unpacked(pack, 1) for pack in (p0, p1, p2, p3)]
    delta_ref[...] = sum(jnp.exp2(part - lse) * delta for part, delta in zip(parts, deltas))
    for j in range(16):
        kt_ref[:, j * BLK : (j + 1) * BLK] = kv_ref[j, :BLK, :].T
    for p in range(4):
        q = q_ref[4 * p : 4 * p + 4].reshape(SPAN, HEAD)
        do = do_ref[4 * p : 4 * p + 4].reshape(SPAN, HEAD)
        lse_now = jnp.concatenate([lse_ref[4 * p + r : 4 * p + r + 1, :] for r in range(4)], axis=1)
        delta_now = jnp.concatenate(
            [delta_ref[4 * p + r : 4 * p + r + 1, :] for r in range(4)], axis=1
        )
        dqt = 0.0
        for i in range(p + 1):
            rows = slice(i * SPAN, (i + 1) * SPAN)
            k = kv_ref[4 * i : 4 * i + 4, :BLK, :].reshape(SPAN, HEAD)
            v = kv_ref[4 * i : 4 * i + 4, BLK:, :].reshape(SPAN, HEAD)
            w = jnp.exp2(mm_nt(k, q) * (SCALE * LOG2E) - lse_now)
            if i == p:
                w = jnp.where(causal(place, p), w, 0.0)
            ds = (w * (mm_nt(v, do) - delta_now)).astype(BF16)
            dv, dk = mm(w.astype(BF16), do), mm(ds, q)
            dv_ref[rows, :] = dv if i == p else dv_ref[rows, :] + dv
            dk_ref[rows, :] = dk if i == p else dk_ref[rows, :] + dk
            dqt = dqt + mm(kt_ref[:, rows], ds)
        dqt_ref[...] = dqt * SCALE
        for x, out in enumerate((dq0, dq1, dq2, dq3)):
            out[p] = dqt_ref[:, block_at(place[1] ^ x)].T.astype(BF16)
    for j in range(16):
        at = slice(j * BLK, (j + 1) * BLK)
        dkv_ref[j, :BLK, :] = (dk_ref[at, :] * SCALE).astype(BF16)
        dkv_ref[j, BLK:, :] = dv_ref[at, :].astype(BF16)


def dq_sum_kernel(place, d0, d1, d2, d3, e0, e1, e2, e3):
    for x, out in enumerate((e0, e1, e2, e3)):
        p = place[0] ^ x
        out[...] = sum(part[p].astype(F32) for part in (d0, d1, d2, d3)).astype(BF16)


def grads_kernel(place, e0, e1, e2, e3, dkv_ref, dq_ref, dk_ref, dv_ref):
    for x, part in enumerate((e0, e1, e2, e3)):
        dq_ref[:, block_at(place[0] ^ x)] = part[...]
    for h in range(4):
        total = sum(dkv_ref[4 * h + i].astype(F32) for i in range(4)).astype(BF16)
        at = slice(h * HEAD, (h + 1) * HEAD)
        dk_ref[:, at] = total[:BLK]
        dv_ref[:, at] = total[BLK:]


def layer_kernel(
    place, a0, a1, a2, a3, w_hbm, kept_hbm, given_hbm, a_ref, rows_ref, w_ref, out_ref,
    a_sem, w_sem, out_sem
):
    parts = [fetch(a.at[place[0]], a_ref.at[x], a_sem.at[x]) for x, a in enumerate((a0, a1, a2, a3))]
    columns = w_columns(place, w_hbm, w_ref, w_sem)
    for x in range(4):
        parts[x].wait()
        rows_ref[:, block_at(place[0] ^ x)] = a_ref[x]
    outs = []
    for x in range(4):
        columns[x].wait()
        out_ref[x] = mm(rows_ref[...], w_ref[x]).astype(BF16)
        out = given_hbm if x & 1 else kept_hbm
        outs.append(fetch(out_ref.at[x], out.at[x >> 1], out_sem.at[x]))
    for out in outs:
        out.wait()


def pair_kernel(place, kept_ref, come_ref, mine_ref, other_ref):
    total = kept_ref[...].astype(F32) + come_ref[...].astype(F32)
    mine_ref[...] = total[0]
    other_ref[...] = total[1].astype(BF16)


def proj_kernel(place, a0, a1, a2, a3, others, cot_ref, out_ref, att_ref):
    for x, part in enumerate((a0, a1, a2, a3)):
        for p in range(4):
            cols = block_at(place[0] ^ x)
            att_ref[block_at(2 * p + place[4 + p]), cols] = part[p]
            att_ref[block_at(2 * p + (place[4 + p] ^ 1)), cols] = others[x, p]
    cot = cot_ref[...].reshape(8 * BLK, 512)
    for i in range(2):
        at = slice(i * 256, (i + 1) * 256)
        total = lax.dot_general(
            cot[:, at], att_ref[...], (((0,), (0,)), ((), ())), preferred_element_type=F32
        )
        out_ref[4 * i : 4 * i + 4] = total.astype(BF16).reshape(4, 64, 512)


def like(*shape, dtype=BF16):
    return jax.ShapeDtypeStruct(shape, dtype)


def params():
    return pltpu.CompilerParams(vmem_limit_bytes=VMEM_LIMIT)


def cost(flops, moved):
    return pl.CostEstimate(flops=int(flops), bytes_accessed=int(moved), transcendentals=0)


def raw(kernel, out_shape, scratch, flops, moved):
    def call(place, *args):
        return pl.pallas_call(
            kernel,
            out_shape=out_shape,
            in_specs=[pl.BlockSpec(memory_space=pltpu.SMEM)]
            + [pl.BlockSpec(memory_space=pltpu.HBM)] * len(args),
            out_specs=[pl.BlockSpec(memory_space=pltpu.HBM)] * len(out_shape),
            scratch_shapes=scratch,
            compiler_params=params(),
            cost_estimate=cost(flops, moved),
        )(place, *args)

    return call


def on_device(kernel, out_shape, scratch, flops, moved):
    def call(place, *args):
        return pl.pallas_call(
            kernel,
            out_shape=out_shape,
            in_specs=[pl.BlockSpec(memory_space=pltpu.SMEM)]
            + [pl.BlockSpec(memory_space=pltpu.VMEM)] * len(args),
            out_specs=[pl.BlockSpec(memory_space=pltpu.VMEM)] * len(out_shape),
            scratch_shapes=scratch,
            compiler_params=params(),
            cost_estimate=cost(flops, moved),
        )(place, *args)

    return call


def per_device(query_rows, key_rows, value_rows, out_proj, cotangent):
    c, f = lax.axis_index("ctx"), lax.axis_index("fsdp")
    p, y, r, z = c // 16, (c // 8) % 2, (c // 2) % 4, c % 2
    place = jnp.stack([p, r, z, f] + [y ^ ((p ^ i) & 1) for i in range(4)]).astype(jnp.int32)
    four = [like(BLK, HEAD)] * 4

    def swap(block, x):
        return lax.ppermute(block, "fsdp", [(i, i ^ x) for i in range(4)])

    far = swap(cotangent, 2)
    *q_pieces, kv_pieces = on_device(prep_kernel, four + [like(16, 2 * BLK, HEAD)], [], 1e6, 2e6)(
        place, query_rows, key_rows, value_rows
    )
    q_mine = jnp.stack(over_heads(q_pieces))
    kv_pieces, far, q_mine = lax.optimization_barrier((kv_pieces, far, q_mine))
    kv = exchange(kv_pieces, key_groups())
    q = over_rows([q_mine] * 4)
    cots = [cotangent, swap(cotangent, 1), far, swap(far, 1)]

    do_pieces, cot_pieces = raw(
        grad_attn_kernel,
        [like(16, BLK, HEAD), like(8, BLK, 512)],
        [
            pltpu.VMEM((4, BLK, 1024), BF16),
            pltpu.VMEM((4, 512, 1024), BF16),
            pltpu.VMEM((16, BLK, HEAD), BF16),
            pltpu.SemaphoreType.DMA((4,)),
            pltpu.SemaphoreType.DMA((4,)),
            pltpu.SemaphoreType.DMA((9,)),
        ],
        5.4e8,
        7e6,
    )(place, *cots, out_proj)
    do_pieces, kv, q = lax.optimization_barrier((do_pieces, kv, q))
    do = exchange(do_pieces, query_groups())

    *o_part, lse_part = on_device(
        fwd_kernel,
        [like(4, BLK, HEAD)] * 4 + [like(16, BLK, dtype=F32)],
        [
            pltpu.VMEM((16, BLK, HEAD), BF16),
            pltpu.VMEM((HEAD, TOKENS), BF16),
            pltpu.VMEM((HEAD, SPAN), F32),
        ],
        2e9,
        2.6e6,
    )(place, *q, kv)

    packs = on_device(
        pack_kernel, [like(SPAN + 96, HEAD)] * 4, [pltpu.VMEM((16, BLK), F32)], 1e6, 1.6e6
    )(place, do, *o_part, lse_part)
    packs, cot_pieces = lax.optimization_barrier((packs, cot_pieces))
    packs = over_rows(packs)
    (att_mine,) = on_device(
        merge_kernel, [like(4, BLK, HEAD)], [pltpu.VMEM((4, 16, BLK), F32)], 1e6, 7e5
    )(place, *packs)
    cot_cols = exchange(cot_pieces, xy_groups())
    packs, att_mine, cot_cols = lax.optimization_barrier((packs, att_mine, cot_cols))
    att = over_heads([att_mine] * 4)

    *dq_part, dkv_part = on_device(
        bwd_kernel,
        [like(4, BLK, HEAD)] * 4 + [like(16, 2 * BLK, HEAD)],
        [
            pltpu.VMEM((16, BLK, HEAD), BF16),
            pltpu.VMEM((HEAD, TOKENS), BF16),
            pltpu.VMEM((16, BLK), F32),
            pltpu.VMEM((16, BLK), F32),
            pltpu.VMEM((HEAD, SPAN), F32),
            pltpu.VMEM((TOKENS, HEAD), F32),
            pltpu.VMEM((TOKENS, HEAD), F32),
        ],
        5e9,
        3.6e6,
    )(place, *q, do, kv, *packs)

    att, cot_cols, dkv_part = lax.optimization_barrier((att, cot_cols, dkv_part))
    dkv_home = exchange(dkv_part, key_groups())
    kept, given = raw(
        layer_kernel,
        [like(2, BLK, 1024)] * 2,
        [
            pltpu.VMEM((4, BLK, HEAD), BF16),
            pltpu.VMEM((BLK, 512), BF16),
            pltpu.VMEM((4, 512, 1024), BF16),
            pltpu.VMEM((4, BLK, 1024), BF16),
            pltpu.SemaphoreType.DMA((4,)),
            pltpu.SemaphoreType.DMA((4,)),
            pltpu.SemaphoreType.DMA((4,)),
        ],
        5.4e8,
        6e6,
    )(place, *att, out_proj)
    (proj_part,) = on_device(
        proj_kernel, [like(8, 64, 512)], [pltpu.VMEM((8 * BLK, 512), BF16)], 5.4e8, 2.6e6
    )(place, *att, hop(jnp.stack(att), 8), cot_cols)
    dq_all = over_rows(dq_part)
    dq_all, proj_part, kept = lax.optimization_barrier((dq_all, proj_part, kept))

    mine, other = on_device(
        pair_kernel, [like(BLK, 1024, dtype=F32), like(BLK, 1024)], [], 1e6, 2e6
    )(place, kept, swap(given, 1))

    proj_part, dkv_home, dq_all = lax.optimization_barrier((proj_part, dkv_home, dq_all))
    proj_home = exchange(proj_part, z_groups())
    dq_pieces = on_device(dq_sum_kernel, four, [], 1e6, 6e5)(place, *dq_all)
    dq_home = over_heads(dq_pieces)
    layer_out = (mine + swap(other, 2).astype(F32)).astype(BF16)
    grad_query, grad_key, grad_value = on_device(
        grads_kernel, [like(BLK, 512)] * 3, [], 1e6, 1.6e6
    )(place, *dq_home, dkv_home)
    proj_grad = jnp.sum(proj_home.astype(F32), axis=0)
    return (layer_out, grad_query, grad_key, grad_value, proj_grad)


def solution(mesh):
    spec = P("ctx", "fsdp")
    return jax.shard_map(
        per_device,
        mesh=mesh,
        in_specs=(spec, spec, spec, P("fsdp", None), spec),
        out_specs=(spec, spec, spec, spec, spec),
        check_vma=False,
    )
```
